512 devices in a mesh: seg: 8 (over x, core), sec: 64 (over z, y).
Axes of the slice: x: 4, y: 4, z: 16, core: 2. Of those that a mesh axis runs over, the one named last changes fastest.
Arguments:
- psi: float32 [8, 8192, 256], P('seg', 'sec'), may hold values from -36 to 36
- left_env: bfloat16 [8, 26, 8192, 128], P('seg', None, 'sec'), may hold values from -3 to 3
- right_env: bfloat16 [8, 26, 256, 256], P('seg'), may hold values from -3 to 3
- term_kind: int32 [26], replicated, may hold values from 0 to 4, as said below
- block_rows: int32 [8, 64], P('seg', 'sec'), may hold values from 16 to 128, as said below
Outputs:
- updated: float32 [8, 8192, 256], P('seg', 'sec')
The draws below stay inside these ranges and needn't reach their ends.
Inputs may be any that keep to these rules, and one draw needn't show every extreme that they name: `term_kind`: each of the five kinds is taken by some MPO index. `block_rows`: in every segment one block is full and one has 16 live rows.
All inputs are finite; a program needn't handle non-finite values.
Results may differ from the reference program's by a relative error of at most 0.01.
Values may be sent and summed in bfloat16 or wider, within the bound.
A program may use at most 64 MiB of HBM per device.

```python
import math
import jax
import jax.numpy as jnp
from jax import lax

W = 26
BLOCK = 128
C = 256
NDN = 8
MIN_ROWS = 16
KRYLOV = 3
SEGS = 8
SECTORS = 64


def mpo_pattern(key):
    key = jax.random.fold_in(key, 7)
    count_key, order_key = jax.random.split(key)
    pair_counts = jax.random.randint(count_key, (2,), 2, 6).astype(jnp.int32)
    first_pairs = pair_counts[0]
    second_pairs = pair_counts[1]
    shuffled = jax.random.permutation(order_key, W).astype(jnp.int32)
    placing = jnp.zeros((W,), jnp.int32).at[shuffled].set(jnp.arange(W, dtype=jnp.int32))
    kind_of = jnp.where(placing < first_pairs, 1, jnp.where(placing < 2 * first_pairs, 2, jnp.where(placing < 2 * first_pairs + second_pairs, 3, jnp.where(placing < 2 * first_pairs + 2 * second_pairs, 4, 0)))).astype(jnp.int32)
    offset = jnp.where(kind_of == 1, first_pairs, jnp.where(kind_of == 2, -first_pairs, jnp.where(kind_of == 3, second_pairs, jnp.where(kind_of == 4, -second_pairs, 0)))).astype(jnp.int32)
    partner = shuffled[placing + offset].astype(jnp.int32)
    hop_count = 2 * (first_pairs + second_pairs)
    onsite_count = W - hop_count
    return (kind_of, partner, onsite_count, hop_count)


def draw_psi(key, part):
    key = jax.random.fold_in(key, 31)
    sector = (jnp.arange(SECTORS * BLOCK) // BLOCK).astype(jnp.float32)
    shape = (SEGS, SECTORS * BLOCK, C)
    base = jnp.clip(jax.random.normal(key, shape, jnp.float32), -6.0, 6.0)
    rise = 6.0 ** (sector / (SECTORS - 1))
    return (base * rise[None, :, None]).astype(jnp.float32)


def draw_left_env(key, part):
    kind_of, partner, onsite_count, hop_count = mpo_pattern(key)
    key = jax.random.fold_in(key, 41)
    onsite_scale = onsite_count.astype(jnp.float32) ** (-0.5)
    hop_scale = 2.5 ** 0.5 * hop_count.astype(jnp.float32) ** (-0.25)
    identity = jnp.eye(BLOCK, dtype=jnp.float32)
    kind_grid = kind_of[:, None, None, None]
    shape = (W, SECTORS, BLOCK, BLOCK)

    def one_segment(index):
        seg_key = jax.random.fold_in(key, index)
        noise_key, extra_key, level_key, mix_key = jax.random.split(seg_key, 4)
        random_part = jnp.clip(jax.random.normal(noise_key, shape, jnp.float32), -6.0, 6.0)
        extra_part = jnp.clip(jax.random.normal(extra_key, shape, jnp.float32), -6.0, 6.0)
        levels = jax.random.uniform(level_key, (W, SECTORS, 1, 1), jnp.float32, 0.6, 1.4)
        mixing = jax.random.uniform(mix_key, (), jnp.float32, 0.0, 0.5 * math.pi)
        symmetric = (random_part + jnp.swapaxes(random_part, 2, 3)) * 0.5 ** 0.5
        onsite = onsite_scale * (levels * identity + 0.5 * symmetric * BLOCK ** (-0.5))
        hopping = hop_scale * random_part * BLOCK ** (-0.5)
        mirrored = jnp.swapaxes(hopping[partner], 2, 3)
        mirrored = jnp.cos(mixing) * mirrored + jnp.sin(mixing) * hop_scale * extra_part * BLOCK ** (-0.5)
        from_lower = jnp.roll(mirrored, 1, axis=1)
        from_upper = jnp.roll(mirrored, NDN, axis=1)
        blocks = jnp.where(kind_grid == 0, onsite, jnp.where(kind_grid == 2, from_lower, jnp.where(kind_grid == 4, from_upper, hopping)))
        return blocks.reshape(W, SECTORS * BLOCK, BLOCK)
    return lax.map(one_segment, jnp.arange(SEGS, dtype=jnp.int32)).astype(jnp.bfloat16)


def draw_right_env(key, part):
    kind_of, partner, onsite_count, hop_count = mpo_pattern(key)
    key = jax.random.fold_in(key, 53)
    noise_key, level_key = jax.random.split(key)
    onsite_scale = onsite_count.astype(jnp.float32) ** (-0.5)
    hop_scale = 2.5 ** 0.5 * hop_count.astype(jnp.float32) ** (-0.25)
    shape = (SEGS, W, C, C)
    random_part = jnp.clip(jax.random.normal(noise_key, shape, jnp.float32), -6.0, 6.0)
    levels = jax.random.uniform(level_key, (SEGS, W, 1, 1), jnp.float32, 0.6, 1.4)
    identity = jnp.eye(C, dtype=jnp.float32)
    symmetric = (random_part + jnp.swapaxes(random_part, 2, 3)) * 0.5 ** 0.5
    onsite = onsite_scale * (levels * identity + 0.5 * symmetric * C ** (-0.5))
    hopping = hop_scale * random_part * C ** (-0.5)
    mirrored = jnp.swapaxes(hopping[:, partner], 2, 3)
    kind_grid = kind_of[None, :, None, None]
    blocks = jnp.where(kind_grid == 0, onsite, jnp.where((kind_grid == 2) | (kind_grid == 4), mirrored, hopping))
    return blocks.astype(jnp.bfloat16)


def draw_term_kind(key, part):
    kind_of, partner, onsite_count, hop_count = mpo_pattern(key)
    return kind_of


def draw_block_rows(key, part):
    key = jax.random.fold_in(key, 23)
    first_key, second_key = jax.random.split(key)
    rows = jax.random.randint(first_key, (SEGS, SECTORS), MIN_ROWS, BLOCK + 1)
    picked = jax.random.randint(second_key, (SEGS,), 0, SECTORS)
    places = jnp.arange(SECTORS, dtype=jnp.int32)[None, :]
    rows = jnp.where(places == picked[:, None], BLOCK, rows)
    rows = jnp.where(places == (picked[:, None] + 1) % SECTORS, MIN_ROWS, rows)
    return rows.astype(jnp.int32)


def setup_inputs(seed: int = 0) -> dict:
    seeds = jax.random.split(jax.random.key(seed), 6)
    return {
        "psi": draw_psi(jax.random.fold_in(seeds[5], 71), 0),
        "left_env": draw_left_env(jax.random.fold_in(seeds[5], 71), 0),
        "right_env": draw_right_env(jax.random.fold_in(seeds[5], 71), 0),
        "term_kind": draw_term_kind(jax.random.fold_in(seeds[5], 71), 0),
        "block_rows": draw_block_rows(jax.random.fold_in(seeds[5], 71), 0),
    }


eps = 1e-06
series_order = 3
step_size = 0.5

def tridiag_coeffs(alphas, betas):
    count = len(alphas)
    diag_part = jnp.diag(jnp.stack(alphas))
    off_part = jnp.diag(jnp.stack(betas), 1) + jnp.diag(jnp.stack(betas), -1)
    matrix = (diag_part + off_part).astype(jnp.float32)
    term = jnp.zeros((count,), jnp.float32).at[0].set(1.0)
    total = term
    for order in range(1, series_order + 1):
        term = lax.optimization_barrier(jnp.sum(matrix * term[None, :], axis=1)) * (-step_size / order)
        total = total + term
    return total

def shifted_sources(blocks):
    sectors = blocks.shape[0]
    grid = blocks.reshape((sectors // NDN, NDN) + blocks.shape[1:])
    zero_col = jnp.zeros_like(grid[:, :1])
    upper = jnp.concatenate([grid[:, 1:], zero_col], axis=1).reshape(blocks.shape)
    lower = jnp.concatenate([zero_col, grid[:, :-1]], axis=1).reshape(blocks.shape)
    zero_row = jnp.zeros_like(blocks[:NDN])
    above = jnp.concatenate([blocks[NDN:], zero_row], axis=0)
    below = jnp.concatenate([zero_row, blocks[:-NDN]], axis=0)
    return jnp.stack([blocks, upper, lower, above, below])

def apply_op(left, vec, right, onehot, mask):
    sources = shifted_sources(vec.astype(jnp.bfloat16)).astype(jnp.float32)
    chosen = jnp.einsum('wk,ksbc->wsbc', onehot, sources).astype(jnp.bfloat16)
    inner_z = jnp.einsum('wsbc,wcd->wsbd', chosen.astype(jnp.float32), right.astype(jnp.float32)).astype(jnp.bfloat16)
    image = jnp.einsum('wsab,wsbd->sad', left.astype(jnp.float32), inner_z.astype(jnp.float32))
    return image * mask

def evolve(left, start, right, onehot, mask):
    count = 1.0 * start.size
    first = start * mask
    norm_start = jnp.sum(first * first) / count
    current = first / jnp.sqrt(norm_start + eps)
    previous = jnp.zeros_like(current)
    beta = jnp.float32(0.0)
    basis = [current]
    alphas = []
    betas = []
    for step in range(KRYLOV):
        image = apply_op(left, current, right, onehot, mask)
        alpha = jnp.sum(current * image) / count
        alphas.append(alpha)
        if step + 1 < KRYLOV:
            remain = image - alpha * current - beta * previous
            beta = jnp.sqrt(jnp.sum(remain * remain) / count + eps)
            betas.append(beta)
            previous = current
            current = remain / beta
            basis.append(current)
    coeffs = tridiag_coeffs(alphas, betas)
    mixed = coeffs[0] * basis[0]
    for index in range(1, KRYLOV):
        mixed = mixed + coeffs[index] * basis[index]
    return mixed / jnp.sqrt(jnp.sum(coeffs * coeffs))

def boundary(first, right):
    scale = (first.shape[2] * first.shape[1] * right.shape[0]) ** (-0.5)
    first_bf = first.astype(jnp.bfloat16).astype(jnp.float32)
    projected = jnp.einsum('sbc,wcd->wsbd', first_bf, right.astype(jnp.float32)).astype(jnp.bfloat16)
    env = jnp.einsum('wsbd,sed->wsbe', projected.astype(jnp.float32), first_bf) * scale
    return env.astype(jnp.bfloat16)

def reference(psi, left_env, right_env, term_kind, block_rows):
    segs, total, cols = psi.shape
    blk = BLOCK
    sectors = total // blk
    onehot = (term_kind[:, None] == jnp.arange(5, dtype=jnp.int32)[None, :]).astype(jnp.float32)
    results = []
    carried = None
    for seg in range(segs):
        rows = jnp.arange(blk, dtype=jnp.int32)[None, :]
        mask = (rows < block_rows[seg][:, None]).astype(jnp.float32)[:, :, None]
        left = left_env[seg].reshape(W, sectors, blk, blk)
        right = right_env[seg]
        first = evolve(left, psi[seg].reshape(sectors, blk, cols), right, onehot, mask)
        if seg > 0:
            left_two = (left.astype(jnp.float32) + carried.astype(jnp.float32)).astype(jnp.bfloat16)
        else:
            left_two = left
        second = evolve(left_two, first, right, onehot, mask)
        carried = boundary(first, right)
        results.append(second.reshape(total, cols))
    return jnp.stack(results)
```

```python
import functools

import jax
import jax.numpy as jnp
from jax import lax
from jax.experimental import pallas as pl
from jax.experimental.pallas import tpu as pltpu
from jax.sharding import PartitionSpec as P

MESH = pl.DeviceIdType.MESH

NDN = 8
KRYLOV = 3
EPS = 1e-06
SERIES_ORDER = 3
STEP_SIZE = 0.5
SHRINK = 2.0**-12
PAIRS = ((0, 0), (0, 1), (0, 2), (0, 3), (1, 1), (1, 2), (1, 3), (2, 2), (2, 3))


def quadratic(gram, first, second):
    total = None
    for i, a in enumerate(first):
        if a is None:
            continue
        inner = None
        for j, b in enumerate(second):
            if b is None:
                continue
            piece = b * gram[(min(i, j), max(i, j))]
            inner = piece if inner is None else inner + piece
        total = a * inner if total is None else total + a * inner
    return total


def coefficients(sums, count):
    norm = sums[(0, 0)] * (1.0 / count) + EPS
    over = 1.0 / norm
    gram = {pair: value * (1.0 / count) * over for pair, value in sums.items()}
    eps = EPS * SHRINK * SHRINK
    a0 = gram[(0, 1)]
    rest = gram[(1, 1)] - 2.0 * a0 * gram[(0, 1)] + a0 * a0 * gram[(0, 0)]
    b1 = jnp.sqrt(jnp.maximum(rest, 0.0) + eps)
    i1 = 1.0 / b1
    v1 = (-a0 * i1, i1)
    w1 = (None, -a0 * i1, i1)
    a1 = quadratic(gram, v1, w1)
    r1 = (-a1 * v1[0] - b1, w1[1] - a1 * v1[1], w1[2])
    rest = quadratic(gram, r1, r1)
    b2 = jnp.sqrt(jnp.maximum(rest, 0.0) + eps)
    i2 = 1.0 / b2
    v2 = tuple(x * i2 for x in r1)
    a2 = quadratic(gram, v2, (None,) + v2)
    a0, a1, a2, b1, b2 = (x * (1.0 / SHRINK) for x in (a0, a1, a2, b1, b2))
    term = (jnp.ones_like(a0), jnp.zeros_like(a0), jnp.zeros_like(a0))
    c = term
    for order in range(1, SERIES_ORDER + 1):
        factor = -STEP_SIZE / order
        term = (
            (a0 * term[0] + b1 * term[1]) * factor,
            (b1 * term[0] + a1 * term[1] + b2 * term[2]) * factor,
            (b2 * term[1] + a2 * term[2]) * factor,
        )
        c = tuple(x + y for x, y in zip(c, term))
    size = jnp.sqrt(c[0] * c[0] + c[1] * c[1] + c[2] * c[2])
    scale = 1.0 / (size * jnp.sqrt(norm))
    return (
        (c[0] + c[1] * v1[0] + c[2] * v2[0]) * scale,
        (c[1] * v1[1] + c[2] * v2[1]) * scale,
        c[2] * v2[2] * scale,
    )


def kernel(
    segs, sectors, kinds, rows, psi, left, right, out,
    r_v, l_v, z_v, src, chosen, u, env_out, env_in, red,
    load_sem, ex_send, ex_recv, red_send, red_recv, env_send, env_recv,
):
    width, blk, cols = l_v.shape[0], psi.shape[0], psi.shape[1]
    grid_rows = sectors // NDN
    seg, sec = lax.axis_index("seg"), lax.axis_index("sec")
    row, col = sec // NDN, sec % NDN
    count = 1.0 * sectors * blk * cols

    loads = [
        pltpu.make_async_copy(right, r_v, load_sem.at[0]),
        pltpu.make_async_copy(left, l_v, load_sem.at[1]),
    ]
    for load in loads:
        load.start()

    barrier = pltpu.get_barrier_semaphore()
    for j in range(1, NDN):
        other = row * NDN + lax.rem(col + j, NDN)
        pl.semaphore_signal(barrier, inc=1, device_id=(seg, other), device_id_type=MESH)
    for j in range(1, grid_rows):
        other = lax.rem(row + j, grid_rows) * NDN + col
        pl.semaphore_signal(barrier, inc=1, device_id=(seg, other), device_id_type=MESH)
    before = lax.rem(seg + segs - 1, segs)
    pl.semaphore_signal(barrier, inc=1, device_id=(before, sec), device_id_type=MESH)

    live = lax.broadcasted_iota(jnp.int32, (blk, cols), 0) < rows[0, 0]
    keep = jnp.where(live, SHRINK, 0.0)
    start = jnp.where(live, psi[...], 0.0)
    u[0] = start
    src[0, 0] = start.astype(jnp.bfloat16)

    neighbours = (
        (1, 1, col < NDN - 1),
        (2, -1, col > 0),
        (3, NDN, row < grid_rows - 1),
        (4, -NDN, row > 0),
    )
    for kind, _, there in neighbours:

        @pl.when(jnp.logical_not(there))
        def _():
            for step in (0, 1, 2, 4, 5):
                src[step, kind] = jnp.zeros((blk, cols), jnp.bfloat16)

    @pl.when(seg == 0)
    def _():
        env_in[...] = jnp.zeros(env_in.shape, env_in.dtype)

    pl.semaphore_wait(barrier, NDN - 1 + grid_rows - 1 + 1)

    def sending(step, kind, offset):
        return pltpu.make_async_remote_copy(
            src_ref=src.at[step, 0],
            dst_ref=src.at[step, kind],
            send_sem=ex_send.at[step, kind],
            recv_sem=ex_recv.at[step, kind],
            device_id=(seg, sec - offset),
            device_id_type=MESH,
        )

    mirrored = {1: col > 0, 2: col < NDN - 1, 3: row > 0, 4: row < grid_rows - 1}

    def exchange_start(step):
        for kind, offset, _ in (neighbours[2], neighbours[3], neighbours[0], neighbours[1]):

            @pl.when(mirrored[kind])
            def _():
                sending(step, kind, offset).start()

    def exchange_wait(step):
        for kind, offset, there in neighbours:

            @pl.when(there)
            def _():
                sending(step, kind, offset).wait_recv()

    def exchange_drain(step):
        for kind, offset, _ in neighbours:

            @pl.when(mirrored[kind])
            def _():
                sending(step, kind, offset).wait_send()

    def right_side(step):
        chosen[...] = src[step]
        for w in range(width):
            source = chosen[kinds[w]]
            z_v[w * blk : (w + 1) * blk, :] = jnp.dot(
                source, r_v[w], preferred_element_type=jnp.float32
            ).astype(jnp.bfloat16)

    def left_side():
        total = jnp.zeros((blk, cols), jnp.float32)
        for w in range(0, width, 2):
            pair = jnp.concatenate([l_v[w], l_v[w + 1]], axis=1)
            total = total + jnp.dot(
                pair, z_v[w * blk : (w + 2) * blk, :], preferred_element_type=jnp.float32
            )
        return total * keep

    def reduce(update):
        lanes = lax.broadcasted_iota(jnp.int32, (16, 128), 1)
        sublanes = lax.broadcasted_iota(jnp.int32, (16, 128), 0)
        parts = []
        for i, j in PAIRS:
            product = u[i] * u[j]
            product = product[:, :128] + product[:, 128:]
            parts.append(jnp.sum(product, axis=0, keepdims=True))
        parts.append(jnp.zeros((16 - len(PAIRS), 128), jnp.float32))
        table = jnp.concatenate(parts, axis=0)
        totals = jnp.sum(table, axis=1, keepdims=True)
        mine = jnp.sum(jnp.where(lanes == sublanes, totals, 0.0), axis=0, keepdims=True)
        for phase, (place, size) in enumerate(((col, NDN), (row, grid_rows))):
            buffer = red.at[update, phase]
            buffer[pl.ds(place, 1), :] = mine

            def passing(j, slot):
                other = lax.rem(place + j, size)
                other = row * NDN + other if phase == 0 else other * NDN + col
                return pltpu.make_async_remote_copy(
                    src_ref=buffer.at[pl.ds(place, 1), :],
                    dst_ref=buffer.at[pl.ds(slot, 1), :],
                    send_sem=red_send.at[update, phase, j],
                    recv_sem=red_recv.at[update, phase, j],
                    device_id=(seg, other),
                    device_id_type=MESH,
                )

            for j in range(1, size):
                passing(j, place).start()
            for j in range(1, size):
                passing(j, lax.rem(place - j + size, size)).wait_recv()
            for j in range(1, size):
                passing(j, place).wait_send()
            mine = jnp.sum(buffer[0:size, :], axis=0, keepdims=True)
        spread = jnp.where(lanes == sublanes, jnp.broadcast_to(mine, (16, 128)), 0.0)
        totals = jnp.broadcast_to(jnp.sum(spread, axis=1, keepdims=True), (16, 128))
        return {pair: totals[k : k + 1, :] for k, pair in enumerate(PAIRS)}

    def widen(coefficient):
        return jnp.concatenate([coefficient] * (cols // 128), axis=1)

    exchange_start(0)
    loads[0].wait()
    loads[1].wait()

    def first_step(step, carry):
        exchange_wait(step)
        right_side(step)
        image = left_side()
        u[step + 1] = image

        @pl.when(step < KRYLOV - 1)
        def _():
            src[step + 1, 0] = image.astype(jnp.bfloat16)
            exchange_start(step + 1)

        return carry

    lax.fori_loop(0, KRYLOV, first_step, 0)
    mix = [widen(x) for x in coefficients(reduce(0), count)]
    first = mix[0] * u[0] + mix[1] * u[1] + mix[2] * u[2]
    first_bf = first.astype(jnp.bfloat16)

    scale = (cols * blk * width) ** (-0.5)
    half = width // 2

    def passing_env(part):
        piece = pl.ds(part * half, half)
        return pltpu.make_async_remote_copy(
            src_ref=env_out.at[piece],
            dst_ref=env_in.at[piece],
            send_sem=env_send.at[part],
            recv_sem=env_recv.at[part],
            device_id=(lax.rem(seg + 1, segs), sec),
            device_id_type=MESH,
        )

    for part in range(2):
        for w in range(part * half, (part + 1) * half):
            projected = jnp.dot(first_bf, r_v[w], preferred_element_type=jnp.float32).astype(jnp.bfloat16)
            env = lax.dot_general(
                projected, first_bf, (((1,), (1,)), ((), ())), preferred_element_type=jnp.float32
            )
            env_out[w] = (env * scale).astype(jnp.bfloat16)

        @pl.when(seg < segs - 1)
        def _():
            passing_env(part).start()

    for kind in range(1, 5):
        mixed = mix[0] * src[0, kind].astype(jnp.float32)
        mixed = mixed + mix[1] * src[1, kind].astype(jnp.float32)
        mixed = mixed + mix[2] * src[2, kind].astype(jnp.float32)
        src[3, kind] = mixed.astype(jnp.bfloat16)
    src[3, 0] = first_bf
    u[0] = first
    right_side(3)

    @pl.when(seg > 0)
    def _():
        passing_env(0).wait_recv()
        passing_env(1).wait_recv()

    for w in range(width):
        l_v[w] = (l_v[w].astype(jnp.float32) + env_in[w].astype(jnp.float32)).astype(jnp.bfloat16)
    image = left_side()
    u[1] = image
    src[4, 0] = image.astype(jnp.bfloat16)
    exchange_start(4)

    def second_step(step, carry):
        exchange_wait(step)
        right_side(step)
        image = left_side()
        u[step - 2] = image

        @pl.when(step < 5)
        def _():
            src[step + 1, 0] = image.astype(jnp.bfloat16)
            exchange_start(step + 1)

        return carry

    lax.fori_loop(4, 6, second_step, 0)
    mix = [widen(x) for x in coefficients(reduce(1), count)]
    out[...] = mix[0] * u[0] + mix[1] * u[1] + mix[2] * u[2]

    for step in (0, 1, 2, 4, 5):
        exchange_drain(step)

    @pl.when(seg < segs - 1)
    def _():
        passing_env(0).wait_send()
        passing_env(1).wait_send()


def per_device(segs, sectors, psi, left_env, right_env, term_kind, block_rows):
    _, blk, cols = psi.shape
    width = left_env.shape[1]
    grid_rows = sectors // NDN
    vmem = pl.BlockSpec(memory_space=pltpu.VMEM)
    smem = pl.BlockSpec(memory_space=pltpu.SMEM)
    anywhere = pl.BlockSpec(memory_space=pl.ANY)
    result = pl.pallas_call(
        functools.partial(kernel, segs, sectors),
        out_shape=jax.ShapeDtypeStruct((blk, cols), jnp.float32),
        in_specs=[smem, smem, vmem, anywhere, anywhere],
        out_specs=vmem,
        scratch_shapes=[
            pltpu.VMEM((width, cols, cols), jnp.bfloat16),
            pltpu.VMEM((width, blk, blk), jnp.bfloat16),
            pltpu.VMEM((width * blk, cols), jnp.bfloat16),
            pltpu.VMEM((6, 5, blk, cols), jnp.bfloat16),
            pltpu.VMEM((5, blk, cols), jnp.bfloat16),
            pltpu.VMEM((KRYLOV + 1, blk, cols), jnp.float32),
            pltpu.VMEM((width, blk, blk), jnp.bfloat16),
            pltpu.VMEM((width, blk, blk), jnp.bfloat16),
            pltpu.VMEM((2, 2, 8, 128), jnp.float32),
            pltpu.SemaphoreType.DMA((2,)),
            pltpu.SemaphoreType.DMA((6, 5)),
            pltpu.SemaphoreType.DMA((6, 5)),
            pltpu.SemaphoreType.DMA((2, 2, max(NDN, grid_rows))),
            pltpu.SemaphoreType.DMA((2, 2, max(NDN, grid_rows))),
            pltpu.SemaphoreType.DMA((2,)),
            pltpu.SemaphoreType.DMA((2,)),
        ],
        compiler_params=pltpu.CompilerParams(
            collective_id=0, has_side_effects=True, vmem_limit_bytes=48 * 2**20
        ),
    )(term_kind, block_rows, psi[0], left_env[0], right_env[0])
    return result[None]


def solution(mesh):
    in_specs = (
        P("seg", "sec", None),
        P("seg", None, "sec", None),
        P("seg", None, None, None),
        P(),
        P("seg", "sec"),
    )
    out_specs = P("seg", "sec", None)
    return jax.shard_map(
        functools.partial(per_device, mesh.shape["seg"], mesh.shape["sec"]),
        mesh=mesh, in_specs=in_specs, out_specs=out_specs, check_vma=False,
    )
```

```python
import functools

import jax
import jax.numpy as jnp
from jax import lax
from jax.experimental import pallas as pl
from jax.experimental.pallas import tpu as pltpu
from jax.sharding import PartitionSpec as P

MESH = pl.DeviceIdType.MESH

NDN = 8
KRYLOV = 3
EPS = 1e-06
SERIES_ORDER = 3
STEP_SIZE = 0.5
VMEM_LIMIT = 63 * 2**20
SHRINK = 2.0**-12
PAIRS = ((0, 0), (0, 1), (0, 2), (0, 3), (1, 1), (1, 2), (1, 3), (2, 2), (2, 3))


def quadratic(gram, first, second):
    total = None
    for i, a in enumerate(first):
        if a is None:
            continue
        inner = None
        for j, b in enumerate(second):
            if b is None:
                continue
            piece = b * gram[(min(i, j), max(i, j))]
            inner = piece if inner is None else inner + piece
        total = a * inner if total is None else total + a * inner
    return total


def coefficients(sums, count):
    norm = sums[(0, 0)] * (1.0 / count) + EPS
    over = 1.0 / norm
    gram = {pair: value * (1.0 / count) * over for pair, value in sums.items()}
    eps = EPS * SHRINK * SHRINK
    a0 = gram[(0, 1)]
    rest = gram[(1, 1)] - 2.0 * a0 * gram[(0, 1)] + a0 * a0 * gram[(0, 0)]
    b1 = jnp.sqrt(jnp.maximum(rest, 0.0) + eps)
    i1 = 1.0 / b1
    v1 = (-a0 * i1, i1)
    w1 = (None, -a0 * i1, i1)
    a1 = quadratic(gram, v1, w1)
    r1 = (-a1 * v1[0] - b1, w1[1] - a1 * v1[1], w1[2])
    rest = quadratic(gram, r1, r1)
    b2 = jnp.sqrt(jnp.maximum(rest, 0.0) + eps)
    i2 = 1.0 / b2
    v2 = tuple(x * i2 for x in r1)
    a2 = quadratic(gram, v2, (None,) + v2)
    a0, a1, a2, b1, b2 = (x * (1.0 / SHRINK) for x in (a0, a1, a2, b1, b2))
    term = (jnp.ones_like(a0), jnp.zeros_like(a0), jnp.zeros_like(a0))
    c = term
    for order in range(1, SERIES_ORDER + 1):
        factor = -STEP_SIZE / order
        term = (
            (a0 * term[0] + b1 * term[1]) * factor,
            (b1 * term[0] + a1 * term[1] + b2 * term[2]) * factor,
            (b2 * term[1] + a2 * term[2]) * factor,
        )
        c = tuple(x + y for x, y in zip(c, term))
    size = jnp.sqrt(c[0] * c[0] + c[1] * c[1] + c[2] * c[2])
    scale = 1.0 / (size * jnp.sqrt(norm))
    return (
        (c[0] + c[1] * v1[0] + c[2] * v2[0]) * scale,
        (c[1] * v1[1] + c[2] * v2[1]) * scale,
        c[2] * v2[2] * scale,
    )


def kernel(
    segs, sectors, kinds_in, rows_in, psi, left, right, out,
    kinds, rows, start_v, r_v, l_v, z_v, src, chosen, u, env_out, env_in, table, red,
    load_sem, ex_send, ex_recv, red_send, red_recv, env_send, env_recv, hello,
):
    width, blk, cols = l_v.shape[0], l_v.shape[1], r_v.shape[2]
    grid_rows = sectors // NDN
    seg, sec = lax.axis_index("seg"), lax.axis_index("sec")
    row, col = sec // NDN, sec % NDN
    count = 1.0 * sectors * blk * cols

    def beside(rows_on):
        return (seg, lax.rem(row + rows_on + grid_rows, grid_rows) * NDN + col)

    loads = [
        pltpu.make_async_copy(psi, start_v, load_sem.at[0]),
        pltpu.make_async_copy(rows_in, rows, load_sem.at[1]),
        pltpu.make_async_copy(kinds_in, kinds, load_sem.at[2]),
        pltpu.make_async_copy(right, r_v, load_sem.at[3]),
        pltpu.make_async_copy(left, l_v, load_sem.at[4]),
    ]
    loads[0].start()
    loads[1].start()

    barrier = pltpu.get_barrier_semaphore()
    for rows_on in (-1, 1):
        pl.semaphore_signal(barrier, inc=1, device_id=beside(rows_on), device_id_type=MESH)
    for j in range(1, NDN):
        other = row * NDN + lax.rem(col + j, NDN)
        pl.semaphore_signal(barrier, inc=1, device_id=(seg, other), device_id_type=MESH)
    before = lax.rem(seg + segs - 1, segs)
    pl.semaphore_signal(barrier, inc=1, device_id=(before, sec), device_id_type=MESH)

    for load in loads[2:]:
        load.start()
    loads[0].wait()
    loads[1].wait()
    live = lax.broadcasted_iota(jnp.int32, (blk, cols), 0) < rows[0, 0]
    start = jnp.where(live, start_v[...], 0.0)
    src[0, 0] = start.astype(jnp.bfloat16)

    pl.semaphore_wait(barrier, 2 + NDN - 1 + 1)

    neighbours = (
        (3, NDN, row < grid_rows - 1),
        (4, -NDN, row > 0),
        (1, 1, col < NDN - 1),
        (2, -1, col > 0),
    )
    mirrored = {1: col > 0, 2: col < NDN - 1, 3: row > 0, 4: row < grid_rows - 1}

    def sending(step, kind, offset):
        return pltpu.make_async_remote_copy(
            src_ref=src.at[step, 0],
            dst_ref=src.at[step, kind],
            send_sem=ex_send.at[step, kind],
            recv_sem=ex_recv.at[step, kind],
            device_id=(seg, sec - offset),
            device_id_type=MESH,
        )

    def exchange_start(step):
        for kind, offset, _ in neighbours:

            @pl.when(mirrored[kind])
            def _():
                sending(step, kind, offset).start()

    def exchange_wait(step):
        for kind, offset, there in neighbours:

            @pl.when(there)
            def _():
                sending(step, kind, offset).wait_recv()

    def exchange_drain(step):
        for kind, offset, _ in neighbours:

            @pl.when(mirrored[kind])
            def _():
                sending(step, kind, offset).wait_send()

    strides = (1, 2, 1)

    def hello_start(turn):
        for rows_on in (-strides[turn], strides[turn]):
            pl.semaphore_signal(hello.at[turn], inc=1, device_id=beside(rows_on), device_id_type=MESH)

    def hello_wait(turn):
        pl.semaphore_wait(hello.at[turn], 2)

    def right_side(step):
        chosen[...] = src[step]
        for w in range(width):
            source = chosen[kinds[w]]
            z_v[w * blk : (w + 1) * blk, :] = jnp.dot(
                source, r_v[w], preferred_element_type=jnp.float32
            ).astype(jnp.bfloat16)

    def left_side():
        total = jnp.zeros((blk, cols), jnp.float32)
        for w in range(0, width, 2):
            pair = jnp.concatenate([l_v[w], l_v[w + 1]], axis=1)
            total = total + jnp.dot(
                pair, z_v[w * blk : (w + 2) * blk, :], preferred_element_type=jnp.float32
            )
        keep = lax.broadcasted_iota(jnp.int32, (blk, cols), 0) < rows[0, 0]
        return total * jnp.where(keep, SHRINK, 0.0)

    def products(last):
        for k, (i, j) in enumerate(PAIRS):
            if j == last:
                product = u[i] * u[j]
                product = product[:, :128] + product[:, 128:]
                table[k : k + 1, :] = jnp.sum(product, axis=0, keepdims=True)

    lanes = lax.broadcasted_iota(jnp.int32, (16, 128), 1)
    sublanes = lax.broadcasted_iota(jnp.int32, (16, 128), 0)

    def reduce(update):
        buffer = red.at[update]
        totals = jnp.sum(table[...], axis=1, keepdims=True)
        mine = jnp.sum(jnp.where(lanes == sublanes, totals, 0.0), axis=0, keepdims=True)
        buffer[pl.ds(sec, 1), :] = mine

        def pass_on(turn, carry):
            far = (turn + 1) // 2
            offset = sectors // 2 + far - 2 * far * lax.rem(turn, 2)
            pltpu.make_async_remote_copy(
                src_ref=buffer.at[pl.ds(sec, 1), :],
                dst_ref=buffer.at[pl.ds(sec, 1), :],
                send_sem=red_send.at[update],
                recv_sem=red_recv.at[update],
                device_id=(seg, lax.rem(sec + offset, sectors)),
                device_id_type=MESH,
            ).start()
            return carry

        lax.fori_loop(0, sectors - 1, pass_on, 0)
        others = buffer.at[pl.ds(0, sectors - 1), :]
        every = pltpu.make_async_remote_copy(
            src_ref=others, dst_ref=others, send_sem=red_send.at[update], recv_sem=red_recv.at[update],
            device_id=(seg, lax.rem(sec + 1, sectors)), device_id_type=MESH,
        )
        every.wait_recv()
        every.wait_send()
        total = jnp.sum(buffer[...], axis=0, keepdims=True)
        spread = jnp.where(lanes == sublanes, jnp.broadcast_to(total, (16, 128)), 0.0)
        totals = jnp.broadcast_to(jnp.sum(spread, axis=1, keepdims=True), (16, 128))
        return {pair: totals[k : k + 1, :] for k, pair in enumerate(PAIRS)}

    def widen(coefficient):
        return jnp.concatenate([coefficient] * (cols // 128), axis=1)

    exchange_start(0)
    hello_start(0)
    u[0] = start
    table[...] = jnp.zeros(table.shape, table.dtype)
    products(0)
    for kind, _, there in neighbours:

        @pl.when(jnp.logical_not(there))
        def _():
            for step in (0, 1, 2, 4, 5):
                src[step, kind] = jnp.zeros((blk, cols), jnp.bfloat16)

    @pl.when(seg == 0)
    def _():
        env_in[...] = jnp.zeros(env_in.shape, env_in.dtype)

    for load in loads[2:]:
        load.wait()

    for step in range(KRYLOV):
        exchange_wait(step)
        hello_wait(step)
        if step + 1 < KRYLOV:
            hello_start(step + 1)
        right_side(step)
        image = left_side()
        if step + 1 < KRYLOV:
            src[step + 1, 0] = image.astype(jnp.bfloat16)
            exchange_start(step + 1)
        u[step + 1] = image
        products(step + 1)

    mix = [widen(x) for x in coefficients(reduce(0), count)]
    first = mix[0] * u[0] + mix[1] * u[1] + mix[2] * u[2]
    first_bf = first.astype(jnp.bfloat16)

    scale = (cols * blk * width) ** (-0.5)
    half = width // 2

    def passing_env(part):
        piece = pl.ds(part * half, half)
        return pltpu.make_async_remote_copy(
            src_ref=env_out.at[piece],
            dst_ref=env_in.at[piece],
            send_sem=env_send.at[part],
            recv_sem=env_recv.at[part],
            device_id=(lax.rem(seg + 1, segs), sec),
            device_id_type=MESH,
        )

    for part in range(2):
        for w in range(part * half, (part + 1) * half):
            projected = jnp.dot(first_bf, r_v[w], preferred_element_type=jnp.float32).astype(jnp.bfloat16)
            env = lax.dot_general(
                projected, first_bf, (((1,), (1,)), ((), ())), preferred_element_type=jnp.float32
            )
            env_out[w] = (env * scale).astype(jnp.bfloat16)

        @pl.when(seg < segs - 1)
        def _():
            passing_env(part).start()

    for kind in range(1, 5):
        mixed = mix[0] * src[0, kind].astype(jnp.float32)
        mixed = mixed + mix[1] * src[1, kind].astype(jnp.float32)
        mixed = mixed + mix[2] * src[2, kind].astype(jnp.float32)
        src[3, kind] = mixed.astype(jnp.bfloat16)
    src[3, 0] = first_bf
    u[0] = first
    right_side(3)
    products(0)

    @pl.when(seg > 0)
    def _():
        passing_env(0).wait_recv()
        passing_env(1).wait_recv()

    for w in range(width):
        l_v[w] = (l_v[w].astype(jnp.float32) + env_in[w].astype(jnp.float32)).astype(jnp.bfloat16)

    for step in range(KRYLOV):
        if step > 0:
            exchange_wait(step + 3)
            right_side(step + 3)
        image = left_side()
        if step + 1 < KRYLOV:
            src[step + 4, 0] = image.astype(jnp.bfloat16)
            exchange_start(step + 4)
        u[step + 1] = image
        products(step + 1)

    mix = [widen(x) for x in coefficients(reduce(1), count)]
    out[...] = mix[0] * u[0] + mix[1] * u[1] + mix[2] * u[2]

    for step in (0, 1, 2, 4, 5):
        exchange_drain(step)

    @pl.when(seg < segs - 1)
    def _():
        passing_env(0).wait_send()
        passing_env(1).wait_send()


def per_device(segs, sectors, psi, left_env, right_env, term_kind, block_rows):
    _, blk, cols = psi.shape
    width = left_env.shape[1]
    anywhere = pl.BlockSpec(memory_space=pl.ANY)
    result = pl.pallas_call(
        functools.partial(kernel, segs, sectors),
        out_shape=jax.ShapeDtypeStruct((blk, cols), jnp.float32),
        in_specs=[anywhere] * 5,
        out_specs=pl.BlockSpec(memory_space=pltpu.VMEM),
        scratch_shapes=[
            pltpu.SMEM((width,), jnp.int32),
            pltpu.SMEM((1, 1), jnp.int32),
            pltpu.VMEM((blk, cols), jnp.float32),
            pltpu.VMEM((width, cols, cols), jnp.bfloat16),
            pltpu.VMEM((width, blk, blk), jnp.bfloat16),
            pltpu.VMEM((width * blk, cols), jnp.bfloat16),
            pltpu.VMEM((6, 5, blk, cols), jnp.bfloat16),
            pltpu.VMEM((5, blk, cols), jnp.bfloat16),
            pltpu.VMEM((KRYLOV + 1, blk, cols), jnp.float32),
            pltpu.VMEM((width, blk, blk), jnp.bfloat16),
            pltpu.VMEM((width, blk, blk), jnp.bfloat16),
            pltpu.VMEM((16, 128), jnp.float32),
            pltpu.VMEM((2, sectors, 128), jnp.float32),
            pltpu.SemaphoreType.DMA((5,)),
            pltpu.SemaphoreType.DMA((6, 5)),
            pltpu.SemaphoreType.DMA((6, 5)),
            pltpu.SemaphoreType.DMA((2,)),
            pltpu.SemaphoreType.DMA((2,)),
            pltpu.SemaphoreType.DMA((2,)),
            pltpu.SemaphoreType.DMA((2,)),
            pltpu.SemaphoreType.REGULAR((3,)),
        ],
        compiler_params=pltpu.CompilerParams(
            collective_id=0, has_side_effects=True, vmem_limit_bytes=VMEM_LIMIT
        ),
    )(term_kind, block_rows, psi[0], left_env[0], right_env[0])
    return result[None]


def solution(mesh):
    in_specs = (
        P("seg", "sec", None),
        P("seg", None, "sec", None),
        P("seg", None, None, None),
        P(),
        P("seg", "sec"),
    )
    out_specs = P("seg", "sec", None)
    return jax.shard_map(
        functools.partial(per_device, mesh.shape["seg"], mesh.shape["sec"]),
        mesh=mesh, in_specs=in_specs, out_specs=out_specs, check_vma=False,
    )
```

```python
import functools

import jax
import jax.numpy as jnp
from jax import lax
from jax.experimental import pallas as pl
from jax.experimental.pallas import tpu as pltpu
from jax.sharding import PartitionSpec as P

MESH = pl.DeviceIdType.MESH

NDN = 8
KRYLOV = 3
EPS = 1e-06
SERIES_ORDER = 3
STEP_SIZE = 0.5
VMEM_LIMIT = 63 * 2**20
SHRINK = 2.0**-12
AHEAD = 20
AHEAD_PARTS = 4
PAIRS = ((0, 0), (0, 1), (0, 2), (0, 3), (1, 1), (1, 2), (1, 3), (2, 2), (2, 3))


def quadratic(gram, first, second):
    total = None
    for i, a in enumerate(first):
        if a is None:
            continue
        inner = None
        for j, b in enumerate(second):
            if b is None:
                continue
            piece = b * gram[(min(i, j), max(i, j))]
            inner = piece if inner is None else inner + piece
        total = a * inner if total is None else total + a * inner
    return total


def coefficients(sums, count):
    norm = sums[(0, 0)] * (1.0 / count) + EPS
    over = 1.0 / norm
    gram = {pair: value * (1.0 / count) * over for pair, value in sums.items()}
    eps = EPS * SHRINK * SHRINK
    a0 = gram[(0, 1)]
    rest = gram[(1, 1)] - 2.0 * a0 * gram[(0, 1)] + a0 * a0 * gram[(0, 0)]
    b1 = jnp.sqrt(jnp.maximum(rest, 0.0) + eps)
    i1 = 1.0 / b1
    v1 = (-a0 * i1, i1)
    w1 = (None, -a0 * i1, i1)
    a1 = quadratic(gram, v1, w1)
    r1 = (-a1 * v1[0] - b1, w1[1] - a1 * v1[1], w1[2])
    rest = quadratic(gram, r1, r1)
    b2 = jnp.sqrt(jnp.maximum(rest, 0.0) + eps)
    i2 = 1.0 / b2
    v2 = tuple(x * i2 for x in r1)
    a2 = quadratic(gram, v2, (None,) + v2)
    a0, a1, a2, b1, b2 = (x * (1.0 / SHRINK) for x in (a0, a1, a2, b1, b2))
    term = (jnp.ones_like(a0), jnp.zeros_like(a0), jnp.zeros_like(a0))
    c = term
    for order in range(1, SERIES_ORDER + 1):
        factor = -STEP_SIZE / order
        term = (
            (a0 * term[0] + b1 * term[1]) * factor,
            (b1 * term[0] + a1 * term[1] + b2 * term[2]) * factor,
            (b2 * term[1] + a2 * term[2]) * factor,
        )
        c = tuple(x + y for x, y in zip(c, term))
    size = jnp.sqrt(c[0] * c[0] + c[1] * c[1] + c[2] * c[2])
    scale = 1.0 / (size * jnp.sqrt(norm))
    return (
        (c[0] + c[1] * v1[0] + c[2] * v2[0]) * scale,
        (c[1] * v1[1] + c[2] * v2[1]) * scale,
        c[2] * v2[2] * scale,
    )


def kernel(
    segs, sectors, kinds_in, rows_in, psi, left, right, out,
    kinds, rows, start_v, r_v, l_v, z_v, src, chosen, u, r_prev, first_prev, env_out, env_in, table, red,
    load_sem, ex_send, ex_recv, red_send, red_recv, ahead_send, ahead_recv, env_send, env_recv, hello,
):
    width, blk, cols = l_v.shape[0], l_v.shape[1], r_v.shape[2]
    grid_rows = sectors // NDN
    seg, sec = lax.axis_index("seg"), lax.axis_index("sec")
    row, col = sec // NDN, sec % NDN
    count = 1.0 * sectors * blk * cols

    def beside(rows_on):
        return (seg, lax.rem(row + rows_on + grid_rows, grid_rows) * NDN + col)

    loads = [
        pltpu.make_async_copy(psi, start_v, load_sem.at[0]),
        pltpu.make_async_copy(rows_in, rows, load_sem.at[1]),
        pltpu.make_async_copy(kinds_in, kinds, load_sem.at[2]),
        pltpu.make_async_copy(right, r_v, load_sem.at[3]),
        pltpu.make_async_copy(left, l_v, load_sem.at[4]),
    ]
    loads[0].start()
    loads[1].start()

    barrier = pltpu.get_barrier_semaphore()
    for rows_on in (-1, 1):
        pl.semaphore_signal(barrier, inc=1, device_id=beside(rows_on), device_id_type=MESH)
    for j in range(1, NDN):
        other = row * NDN + lax.rem(col + j, NDN)
        pl.semaphore_signal(barrier, inc=1, device_id=(seg, other), device_id_type=MESH)
    before = lax.rem(seg + segs - 1, segs)
    pl.semaphore_signal(barrier, inc=1, device_id=(before, sec), device_id_type=MESH)

    for load in loads[2:]:
        load.start()
    loads[0].wait()
    loads[1].wait()
    live = lax.broadcasted_iota(jnp.int32, (blk, cols), 0) < rows[0, 0]
    start = jnp.where(live, start_v[...], 0.0)
    src[0, 0] = start.astype(jnp.bfloat16)

    pl.semaphore_wait(barrier, 2 + NDN - 1 + 1)

    neighbours = (
        (3, NDN, row < grid_rows - 1),
        (4, -NDN, row > 0),
        (1, 1, col < NDN - 1),
        (2, -1, col > 0),
    )
    mirrored = {1: col > 0, 2: col < NDN - 1, 3: row > 0, 4: row < grid_rows - 1}

    def sending(step, kind, offset):
        return pltpu.make_async_remote_copy(
            src_ref=src.at[step, 0],
            dst_ref=src.at[step, kind],
            send_sem=ex_send.at[step, kind],
            recv_sem=ex_recv.at[step, kind],
            device_id=(seg, sec - offset),
            device_id_type=MESH,
        )

    def exchange_start(step):
        for kind, offset, _ in neighbours:

            @pl.when(mirrored[kind])
            def _():
                sending(step, kind, offset).start()

    def exchange_wait(step):
        for kind, offset, there in neighbours:

            @pl.when(there)
            def _():
                sending(step, kind, offset).wait_recv()

    def exchange_drain(step):
        for kind, offset, _ in neighbours:

            @pl.when(mirrored[kind])
            def _():
                sending(step, kind, offset).wait_send()

    strides = (1, 2, 1)

    def hello_start(turn):
        for rows_on in (-strides[turn], strides[turn]):
            pl.semaphore_signal(hello.at[turn], inc=1, device_id=beside(rows_on), device_id_type=MESH)

    def hello_wait(turn):
        pl.semaphore_wait(hello.at[turn], 2)

    def right_side(step):
        chosen[...] = src[step]
        for w in range(width):
            source = chosen[kinds[w]]
            z_v[w * blk : (w + 1) * blk, :] = jnp.dot(
                source, r_v[w], preferred_element_type=jnp.float32
            ).astype(jnp.bfloat16)

    def left_side():
        total = jnp.zeros((blk, cols), jnp.float32)
        for w in range(0, width, 2):
            pair = jnp.concatenate([l_v[w], l_v[w + 1]], axis=1)
            total = total + jnp.dot(
                pair, z_v[w * blk : (w + 2) * blk, :], preferred_element_type=jnp.float32
            )
        keep = lax.broadcasted_iota(jnp.int32, (blk, cols), 0) < rows[0, 0]
        return total * jnp.where(keep, SHRINK, 0.0)

    def products(last):
        for k, (i, j) in enumerate(PAIRS):
            if j == last:
                product = u[i] * u[j]
                product = product[:, :128] + product[:, 128:]
                table[k : k + 1, :] = jnp.sum(product, axis=0, keepdims=True)

    lanes = lax.broadcasted_iota(jnp.int32, (16, 128), 1)
    sublanes = lax.broadcasted_iota(jnp.int32, (16, 128), 0)

    def reduce(update):
        buffer = red.at[update]
        totals = jnp.sum(table[...], axis=1, keepdims=True)
        mine = jnp.sum(jnp.where(lanes == sublanes, totals, 0.0), axis=0, keepdims=True)
        buffer[pl.ds(sec, 1), :] = mine

        def pass_on(turn, carry):
            far = (turn + 1) // 2
            offset = sectors // 2 + far - 2 * far * lax.rem(turn, 2)
            pltpu.make_async_remote_copy(
                src_ref=buffer.at[pl.ds(sec, 1), :],
                dst_ref=buffer.at[pl.ds(sec, 1), :],
                send_sem=red_send.at[update],
                recv_sem=red_recv.at[update],
                device_id=(seg, lax.rem(sec + offset, sectors)),
                device_id_type=MESH,
            ).start()
            return carry

        lax.fori_loop(0, sectors - 1, pass_on, 0)
        others = buffer.at[pl.ds(0, sectors - 1), :]
        every = pltpu.make_async_remote_copy(
            src_ref=others, dst_ref=others, send_sem=red_send.at[update], recv_sem=red_recv.at[update],
            device_id=(seg, lax.rem(sec + 1, sectors)), device_id_type=MESH,
        )
        every.wait_recv()
        every.wait_send()
        total = jnp.sum(buffer[...], axis=0, keepdims=True)
        spread = jnp.where(lanes == sublanes, jnp.broadcast_to(total, (16, 128)), 0.0)
        totals = jnp.broadcast_to(jnp.sum(spread, axis=1, keepdims=True), (16, 128))
        return {pair: totals[k : k + 1, :] for k, pair in enumerate(PAIRS)}

    def widen(coefficient):
        return jnp.concatenate([coefficient] * (cols // 128), axis=1)

    following = (lax.rem(seg + 1, segs), sec)
    ahead = min(AHEAD, width - 2)
    bounds = [ahead * part // AHEAD_PARTS for part in range(AHEAD_PARTS + 1)]

    def passing_right(part):
        piece = pl.ds(bounds[part], bounds[part + 1] - bounds[part])
        return pltpu.make_async_remote_copy(
            src_ref=right.at[piece], dst_ref=r_prev.at[piece],
            send_sem=ahead_send.at[part], recv_sem=ahead_recv.at[part],
            device_id=following, device_id_type=MESH,
        )

    def passing_first():
        return pltpu.make_async_remote_copy(
            src_ref=src.at[3, 0], dst_ref=first_prev, send_sem=env_send.at[0], recv_sem=env_recv.at[0],
            device_id=following, device_id_type=MESH,
        )

    def passing_env():
        return pltpu.make_async_remote_copy(
            src_ref=env_out, dst_ref=env_in, send_sem=env_send.at[1], recv_sem=env_recv.at[1],
            device_id=following, device_id_type=MESH,
        )

    def boundary(vector, block):
        projected = jnp.dot(vector, block, preferred_element_type=jnp.float32).astype(jnp.bfloat16)
        env = lax.dot_general(projected, vector, (((1,), (1,)), ((), ())), preferred_element_type=jnp.float32)
        return (env * (cols * blk * width) ** (-0.5)).astype(jnp.bfloat16)

    exchange_start(0)

    @pl.when(seg < segs - 1)
    def _():
        for part in range(AHEAD_PARTS):
            passing_right(part).start()

    hello_start(0)
    u[0] = start
    table[...] = jnp.zeros(table.shape, table.dtype)
    products(0)
    for kind, _, there in neighbours:

        @pl.when(jnp.logical_not(there))
        def _():
            for step in (0, 1, 2, 4, 5):
                src[step, kind] = jnp.zeros((blk, cols), jnp.bfloat16)

    for load in loads[2:]:
        load.wait()

    for step in range(KRYLOV):
        exchange_wait(step)
        hello_wait(step)
        if step + 1 < KRYLOV:
            hello_start(step + 1)
        right_side(step)
        image = left_side()
        if step + 1 < KRYLOV:
            src[step + 1, 0] = image.astype(jnp.bfloat16)
            exchange_start(step + 1)
        u[step + 1] = image
        products(step + 1)

    mix = [widen(x) for x in coefficients(reduce(0), count)]
    first = mix[0] * u[0] + mix[1] * u[1] + mix[2] * u[2]
    first_bf = first.astype(jnp.bfloat16)

    src[3, 0] = first_bf

    @pl.when(seg < segs - 1)
    def _():
        passing_first().start()
        for w in range(ahead, width):
            env_out[w - ahead] = boundary(first_bf, r_v[w])
        passing_env().start()

    for kind in range(1, 5):
        mixed = mix[0] * src[0, kind].astype(jnp.float32)
        mixed = mixed + mix[1] * src[1, kind].astype(jnp.float32)
        mixed = mixed + mix[2] * src[2, kind].astype(jnp.float32)
        src[3, kind] = mixed.astype(jnp.bfloat16)
    u[0] = first
    right_side(3)
    products(0)

    @pl.when(seg > 0)
    def _():
        for part in range(AHEAD_PARTS):
            passing_right(part).wait_recv()
        passing_first().wait_recv()
        vector = first_prev[...]
        for w in range(ahead):
            env = boundary(vector, r_prev[w])
            l_v[w] = (l_v[w].astype(jnp.float32) + env.astype(jnp.float32)).astype(jnp.bfloat16)
        passing_env().wait_recv()
        for w in range(ahead, width):
            env = env_in[w - ahead]
            l_v[w] = (l_v[w].astype(jnp.float32) + env.astype(jnp.float32)).astype(jnp.bfloat16)

    for step in range(KRYLOV):
        if step > 0:
            exchange_wait(step + 3)
            right_side(step + 3)
        image = left_side()
        if step + 1 < KRYLOV:
            src[step + 4, 0] = image.astype(jnp.bfloat16)
            exchange_start(step + 4)
        u[step + 1] = image
        products(step + 1)

    mix = [widen(x) for x in coefficients(reduce(1), count)]
    out[...] = mix[0] * u[0] + mix[1] * u[1] + mix[2] * u[2]

    for step in (0, 1, 2, 4, 5):
        exchange_drain(step)

    @pl.when(seg < segs - 1)
    def _():
        for part in range(AHEAD_PARTS):
            passing_right(part).wait_send()
        passing_first().wait_send()
        passing_env().wait_send()


def per_device(segs, sectors, psi, left_env, right_env, term_kind, block_rows):
    _, blk, cols = psi.shape
    width = left_env.shape[1]
    ahead = min(AHEAD, width - 2)
    anywhere = pl.BlockSpec(memory_space=pl.ANY)
    result = pl.pallas_call(
        functools.partial(kernel, segs, sectors),
        out_shape=jax.ShapeDtypeStruct((blk, cols), jnp.float32),
        in_specs=[anywhere] * 5,
        out_specs=pl.BlockSpec(memory_space=pltpu.VMEM),
        scratch_shapes=[
            pltpu.SMEM((width,), jnp.int32),
            pltpu.SMEM((1, 1), jnp.int32),
            pltpu.VMEM((blk, cols), jnp.float32),
            pltpu.VMEM((width, cols, cols), jnp.bfloat16),
            pltpu.VMEM((width, blk, blk), jnp.bfloat16),
            pltpu.VMEM((width * blk, cols), jnp.bfloat16),
            pltpu.VMEM((6, 5, blk, cols), jnp.bfloat16),
            pltpu.VMEM((5, blk, cols), jnp.bfloat16),
            pltpu.VMEM((KRYLOV + 1, blk, cols), jnp.float32),
            pltpu.VMEM((ahead, cols, cols), jnp.bfloat16),
            pltpu.VMEM((blk, cols), jnp.bfloat16),
            pltpu.VMEM((width - ahead, blk, blk), jnp.bfloat16),
            pltpu.VMEM((width - ahead, blk, blk), jnp.bfloat16),
            pltpu.VMEM((16, 128), jnp.float32),
            pltpu.VMEM((2, sectors, 128), jnp.float32),
            pltpu.SemaphoreType.DMA((5,)),
            pltpu.SemaphoreType.DMA((6, 5)),
            pltpu.SemaphoreType.DMA((6, 5)),
            pltpu.SemaphoreType.DMA((2,)),
            pltpu.SemaphoreType.DMA((2,)),
            pltpu.SemaphoreType.DMA((AHEAD_PARTS,)),
            pltpu.SemaphoreType.DMA((AHEAD_PARTS,)),
            pltpu.SemaphoreType.DMA((2,)),
            pltpu.SemaphoreType.DMA((2,)),
            pltpu.SemaphoreType.REGULAR((3,)),
        ],
        compiler_params=pltpu.CompilerParams(
            collective_id=0, has_side_effects=True, vmem_limit_bytes=VMEM_LIMIT
        ),
    )(term_kind, block_rows, psi[0], left_env[0], right_env[0])
    return result[None]


def solution(mesh):
    in_specs = (
        P("seg", "sec", None),
        P("seg", None, "sec", None),
        P("seg", None, None, None),
        P(),
        P("seg", "sec"),
    )
    out_specs = P("seg", "sec", None)
    return jax.shard_map(
        functools.partial(per_device, mesh.shape["seg"], mesh.shape["sec"]),
        mesh=mesh, in_specs=in_specs, out_specs=out_specs, check_vma=False,
    )
```

```python
import functools

import jax
import jax.numpy as jnp
from jax import lax
from jax.experimental import pallas as pl
from jax.experimental.pallas import tpu as pltpu
from jax.sharding import PartitionSpec as P

MESH = pl.DeviceIdType.MESH

NDN = 8
KRYLOV = 3
EPS = 1e-06
SERIES_ORDER = 3
STEP_SIZE = 0.5
VMEM_LIMIT = 63 * 2**20
SHRINK = 2.0**-12
AHEAD = 20
AHEAD_PARTS = 4
PAIRS = ((0, 0), (0, 1), (0, 2), (0, 3), (1, 1), (1, 2), (1, 3), (2, 2), (2, 3))


def quadratic(gram, first, second):
    total = None
    for i, a in enumerate(first):
        if a is None:
            continue
        inner = None
        for j, b in enumerate(second):
            if b is None:
                continue
            piece = b * gram[(min(i, j), max(i, j))]
            inner = piece if inner is None else inner + piece
        total = a * inner if total is None else total + a * inner
    return total


def coefficients(sums, count):
    norm = sums[(0, 0)] * (1.0 / count) + EPS
    over = 1.0 / norm
    gram = {pair: value * (1.0 / count) * over for pair, value in sums.items()}
    eps = EPS * SHRINK * SHRINK
    a0 = gram[(0, 1)]
    rest = gram[(1, 1)] - 2.0 * a0 * gram[(0, 1)] + a0 * a0 * gram[(0, 0)]
    b1 = jnp.sqrt(jnp.maximum(rest, 0.0) + eps)
    i1 = 1.0 / b1
    v1 = (-a0 * i1, i1)
    w1 = (None, -a0 * i1, i1)
    a1 = quadratic(gram, v1, w1)
    r1 = (-a1 * v1[0] - b1, w1[1] - a1 * v1[1], w1[2])
    rest = quadratic(gram, r1, r1)
    b2 = jnp.sqrt(jnp.maximum(rest, 0.0) + eps)
    i2 = 1.0 / b2
    v2 = tuple(x * i2 for x in r1)
    a2 = quadratic(gram, v2, (None,) + v2)
    a0, a1, a2, b1, b2 = (x * (1.0 / SHRINK) for x in (a0, a1, a2, b1, b2))
    term = (jnp.ones_like(a0), jnp.zeros_like(a0), jnp.zeros_like(a0))
    c = term
    for order in range(1, SERIES_ORDER + 1):
        factor = -STEP_SIZE / order
        term = (
            (a0 * term[0] + b1 * term[1]) * factor,
            (b1 * term[0] + a1 * term[1] + b2 * term[2]) * factor,
            (b2 * term[1] + a2 * term[2]) * factor,
        )
        c = tuple(x + y for x, y in zip(c, term))
    size = jnp.sqrt(c[0] * c[0] + c[1] * c[1] + c[2] * c[2])
    scale = 1.0 / (size * jnp.sqrt(norm))
    return (
        (c[0] + c[1] * v1[0] + c[2] * v2[0]) * scale,
        (c[1] * v1[1] + c[2] * v2[1]) * scale,
        c[2] * v2[2] * scale,
    )


def kernel(
    segs, sectors, kinds_in, rows_in, psi, left, right, out,
    kinds, rows, start_v, r_v, l_v, z_v, src_0, src_1, src_2, src_3, src_4, src_5, u, r_prev, first_prev, env_out, env_in, table, red,
    load_sem, ex_send, ex_recv, red_send, red_recv, ahead_send, ahead_recv, env_send, env_recv, hello,
):
    src = (src_0, src_1, src_2, src_3, src_4, src_5)
    width, blk, cols = l_v.shape[0], l_v.shape[1], r_v.shape[2]
    grid_rows = sectors // NDN
    seg, sec = lax.axis_index("seg"), lax.axis_index("sec")
    row, col = sec // NDN, sec % NDN
    count = 1.0 * sectors * blk * cols

    def beside(rows_on):
        return (seg, lax.rem(row + rows_on + grid_rows, grid_rows) * NDN + col)

    def along(columns_on):
        return (seg, row * NDN + lax.rem(col + columns_on + NDN, NDN))

    loads = [
        pltpu.make_async_copy(psi, start_v, load_sem.at[0]),
        pltpu.make_async_copy(rows_in, rows, load_sem.at[1]),
        pltpu.make_async_copy(kinds_in, kinds, load_sem.at[2]),
        pltpu.make_async_copy(right, r_v, load_sem.at[3]),
        pltpu.make_async_copy(left, l_v, load_sem.at[4]),
    ]
    loads[0].start()
    loads[1].start()

    barrier = pltpu.get_barrier_semaphore()
    for on in (-1, 1):
        pl.semaphore_signal(barrier, inc=1, device_id=beside(on), device_id_type=MESH)
        pl.semaphore_signal(barrier, inc=1, device_id=along(on), device_id_type=MESH)
    before = lax.rem(seg + segs - 1, segs)
    pl.semaphore_signal(barrier, inc=1, device_id=(before, sec), device_id_type=MESH)

    for load in loads[2:]:
        load.start()
    loads[0].wait()
    loads[1].wait()
    live = lax.broadcasted_iota(jnp.int32, (blk, cols), 0) < rows[0, 0]
    start = jnp.where(live, start_v[...], 0.0)
    src[0][0] = start.astype(jnp.bfloat16)

    pl.semaphore_wait(barrier, 4 + 1)

    neighbours = (
        (1, 1, col < NDN - 1),
        (2, -1, col > 0),
        (3, NDN, row < grid_rows - 1),
        (4, -NDN, row > 0),
    )
    mirrored = {1: col > 0, 2: col < NDN - 1, 3: row > 0, 4: row < grid_rows - 1}

    def sending(step, kind, offset):
        return pltpu.make_async_remote_copy(
            src_ref=src[step].at[0],
            dst_ref=src[step].at[kind],
            send_sem=ex_send.at[step, kind],
            recv_sem=ex_recv.at[step, kind],
            device_id=(seg, sec - offset),
            device_id_type=MESH,
        )

    def exchange_start(step):
        for kind, offset, _ in neighbours:

            @pl.when(mirrored[kind])
            def _():
                sending(step, kind, offset).start()

    def exchange_wait(step):
        for kind, offset, there in neighbours:

            @pl.when(there)
            def _():
                sending(step, kind, offset).wait_recv()

    def exchange_drain(step):
        for kind, offset, _ in neighbours:

            @pl.when(mirrored[kind])
            def _():
                sending(step, kind, offset).wait_send()

    rounds = ((1, True), (2, True), (1, False), (2, False), (1, False))

    def hello_start(turn):
        stride, both = rounds[turn]
        for on in (-stride, stride):
            pl.semaphore_signal(hello.at[turn], inc=1, device_id=beside(on), device_id_type=MESH)
            if both:
                pl.semaphore_signal(hello.at[turn], inc=1, device_id=along(on), device_id_type=MESH)

    def hello_wait(turn):
        pl.semaphore_wait(hello.at[turn], 4 if rounds[turn][1] else 2)

    def hello_next(turn):
        hello_wait(turn)
        if turn + 1 < len(rounds):
            hello_start(turn + 1)

    def right_side(step):
        for w in range(width):
            source = src[step][kinds[w]]
            z_v[w * blk : (w + 1) * blk, :] = jnp.dot(
                source, r_v[w], preferred_element_type=jnp.float32
            ).astype(jnp.bfloat16)

    def left_side():
        total = jnp.zeros((blk, cols), jnp.float32)
        for w in range(0, width, 2):
            pair = jnp.concatenate([l_v[w], l_v[w + 1]], axis=1)
            total = total + jnp.dot(
                pair, z_v[w * blk : (w + 2) * blk, :], preferred_element_type=jnp.float32
            )
        keep = lax.broadcasted_iota(jnp.int32, (blk, cols), 0) < rows[0, 0]
        return total * jnp.where(keep, SHRINK, 0.0)

    def products(last):
        for k, (i, j) in enumerate(PAIRS):
            if j == last:
                product = u[i] * u[j]
                product = product[:, :128] + product[:, 128:]
                table[k : k + 1, :] = jnp.sum(product, axis=0, keepdims=True)

    lanes = lax.broadcasted_iota(jnp.int32, (16, 128), 1)
    sublanes = lax.broadcasted_iota(jnp.int32, (16, 128), 0)

    def reduce(update):
        buffer = red.at[update]
        totals = jnp.sum(table[...], axis=1, keepdims=True)
        mine = jnp.sum(jnp.where(lanes == sublanes, totals, 0.0), axis=0, keepdims=True)
        buffer[pl.ds(sec, 1), :] = mine

        def pass_on(turn, carry):
            far = (turn + 1) // 2
            offset = sectors // 2 + far - 2 * far * lax.rem(turn, 2)
            pltpu.make_async_remote_copy(
                src_ref=buffer.at[pl.ds(sec, 1), :],
                dst_ref=buffer.at[pl.ds(sec, 1), :],
                send_sem=red_send.at[update],
                recv_sem=red_recv.at[update],
                device_id=(seg, lax.rem(sec + offset, sectors)),
                device_id_type=MESH,
            ).start()
            return carry

        lax.fori_loop(0, sectors - 1, pass_on, 0)
        others = buffer.at[pl.ds(0, sectors - 1), :]
        every = pltpu.make_async_remote_copy(
            src_ref=others, dst_ref=others, send_sem=red_send.at[update], recv_sem=red_recv.at[update],
            device_id=(seg, lax.rem(sec + 1, sectors)), device_id_type=MESH,
        )
        every.wait_recv()
        every.wait_send()
        total = jnp.sum(buffer[...], axis=0, keepdims=True)
        spread = jnp.where(lanes == sublanes, jnp.broadcast_to(total, (16, 128)), 0.0)
        totals = jnp.broadcast_to(jnp.sum(spread, axis=1, keepdims=True), (16, 128))
        return {pair: totals[k : k + 1, :] for k, pair in enumerate(PAIRS)}

    def widen(coefficient):
        return jnp.concatenate([coefficient] * (cols // 128), axis=1)

    following = (lax.rem(seg + 1, segs), sec)
    ahead = min(AHEAD, width - 2)
    bounds = [ahead * part // AHEAD_PARTS for part in range(AHEAD_PARTS + 1)]

    def passing_right(part):
        piece = pl.ds(bounds[part], bounds[part + 1] - bounds[part])
        return pltpu.make_async_remote_copy(
            src_ref=right.at[piece], dst_ref=r_prev.at[piece],
            send_sem=ahead_send.at[part], recv_sem=ahead_recv.at[part],
            device_id=following, device_id_type=MESH,
        )

    def passing_first():
        return pltpu.make_async_remote_copy(
            src_ref=src[3].at[0], dst_ref=first_prev, send_sem=env_send.at[0], recv_sem=env_recv.at[0],
            device_id=following, device_id_type=MESH,
        )

    def passing_env():
        return pltpu.make_async_remote_copy(
            src_ref=env_out, dst_ref=env_in, send_sem=env_send.at[1], recv_sem=env_recv.at[1],
            device_id=following, device_id_type=MESH,
        )

    def boundary(vector, block):
        projected = jnp.dot(vector, block, preferred_element_type=jnp.float32).astype(jnp.bfloat16)
        env = lax.dot_general(projected, vector, (((1,), (1,)), ((), ())), preferred_element_type=jnp.float32)
        return (env * (cols * blk * width) ** (-0.5)).astype(jnp.bfloat16)

    exchange_start(0)

    @pl.when(seg < segs - 1)
    def _():
        for part in range(AHEAD_PARTS):
            passing_right(part).start()

    hello_start(0)
    u[0] = start
    table[...] = jnp.zeros(table.shape, table.dtype)
    products(0)
    for kind, _, there in neighbours:

        @pl.when(jnp.logical_not(there))
        def _():
            for step in (0, 1, 2, 4, 5):
                src[step][kind] = jnp.zeros((blk, cols), jnp.bfloat16)

    for load in loads[2:]:
        load.wait()

    for step in range(KRYLOV):
        hello_next(2 * step)
        exchange_wait(step)
        right_side(step)
        image = left_side()
        if step + 1 < KRYLOV:
            src[step + 1][0] = image.astype(jnp.bfloat16)
            exchange_start(step + 1)
            hello_next(2 * step + 1)
        u[step + 1] = image
        products(step + 1)

    mix = [widen(x) for x in coefficients(reduce(0), count)]
    first = mix[0] * u[0] + mix[1] * u[1] + mix[2] * u[2]
    first_bf = first.astype(jnp.bfloat16)

    src[3][0] = first_bf

    @pl.when(seg < segs - 1)
    def _():
        passing_first().start()
        for w in range(ahead, width):
            env_out[w - ahead] = boundary(first_bf, r_v[w])
        passing_env().start()

    for kind in range(1, 5):
        mixed = mix[0] * src[0][kind].astype(jnp.float32)
        mixed = mixed + mix[1] * src[1][kind].astype(jnp.float32)
        mixed = mixed + mix[2] * src[2][kind].astype(jnp.float32)
        src[3][kind] = mixed.astype(jnp.bfloat16)
    u[0] = first
    right_side(3)
    products(0)

    @pl.when(seg > 0)
    def _():
        for part in range(AHEAD_PARTS):
            passing_right(part).wait_recv()
        passing_first().wait_recv()
        vector = first_prev[...]
        for w in range(ahead):
            env = boundary(vector, r_prev[w])
            l_v[w] = (l_v[w].astype(jnp.float32) + env.astype(jnp.float32)).astype(jnp.bfloat16)
        passing_env().wait_recv()
        for w in range(ahead, width):
            env = env_in[w - ahead]
            l_v[w] = (l_v[w].astype(jnp.float32) + env.astype(jnp.float32)).astype(jnp.bfloat16)

    for step in range(KRYLOV):
        if step > 0:
            exchange_wait(step + 3)
            right_side(step + 3)
        image = left_side()
        if step + 1 < KRYLOV:
            src[step + 4][0] = image.astype(jnp.bfloat16)
            exchange_start(step + 4)
        u[step + 1] = image
        products(step + 1)

    mix = [widen(x) for x in coefficients(reduce(1), count)]
    out[...] = mix[0] * u[0] + mix[1] * u[1] + mix[2] * u[2]

    for step in (0, 1, 2, 4, 5):
        exchange_drain(step)

    @pl.when(seg < segs - 1)
    def _():
        for part in range(AHEAD_PARTS):
            passing_right(part).wait_send()
        passing_first().wait_send()
        passing_env().wait_send()


def per_device(segs, sectors, psi, left_env, right_env, term_kind, block_rows):
    _, blk, cols = psi.shape
    width = left_env.shape[1]
    ahead = min(AHEAD, width - 2)
    anywhere = pl.BlockSpec(memory_space=pltpu.HBM)
    result = pl.pallas_call(
        functools.partial(kernel, segs, sectors),
        out_shape=pltpu.VMEM((blk, cols), jnp.float32),
        in_specs=[anywhere] * 5,
        out_specs=pl.BlockSpec(memory_space=pltpu.VMEM),
        scratch_shapes=[
            pltpu.SMEM((width,), jnp.int32),
            pltpu.SMEM((1, 1), jnp.int32),
            pltpu.VMEM((blk, cols), jnp.float32),
            pltpu.VMEM((width, cols, cols), jnp.bfloat16),
            pltpu.VMEM((width, blk, blk), jnp.bfloat16),
            pltpu.VMEM((width * blk, cols), jnp.bfloat16),
            *[pltpu.VMEM((5, blk, cols), jnp.bfloat16) for _ in range(6)],
            pltpu.VMEM((KRYLOV + 1, blk, cols), jnp.float32),
            pltpu.VMEM((ahead, cols, cols), jnp.bfloat16),
            pltpu.VMEM((blk, cols), jnp.bfloat16),
            pltpu.VMEM((width - ahead, blk, blk), jnp.bfloat16),
            pltpu.VMEM((width - ahead, blk, blk), jnp.bfloat16),
            pltpu.VMEM((16, 128), jnp.float32),
            pltpu.VMEM((2, sectors, 128), jnp.float32),
            pltpu.SemaphoreType.DMA((5,)),
            pltpu.SemaphoreType.DMA((6, 5)),
            pltpu.SemaphoreType.DMA((6, 5)),
            pltpu.SemaphoreType.DMA((2,)),
            pltpu.SemaphoreType.DMA((2,)),
            pltpu.SemaphoreType.DMA((AHEAD_PARTS,)),
            pltpu.SemaphoreType.DMA((AHEAD_PARTS,)),
            pltpu.SemaphoreType.DMA((2,)),
            pltpu.SemaphoreType.DMA((2,)),
            pltpu.SemaphoreType.REGULAR((5,)),
        ],
        compiler_params=pltpu.CompilerParams(
            collective_id=0, has_side_effects=True, vmem_limit_bytes=VMEM_LIMIT
        ),
    )(term_kind, block_rows, psi[0], left_env[0], right_env[0])
    return result[None]


def solution(mesh):
    in_specs = (
        P("seg", "sec", None),
        P("seg", None, "sec", None),
        P("seg", None, None, None),
        P(),
        P("seg", "sec"),
    )
    out_specs = P("seg", "sec", None)
    return jax.shard_map(
        functools.partial(per_device, mesh.shape["seg"], mesh.shape["sec"]),
        mesh=mesh, in_specs=in_specs, out_specs=out_specs, check_vma=False,
    )
```

```python
import functools

import jax
import jax.numpy as jnp
from jax import lax
from jax.experimental import pallas as pl
from jax.experimental.pallas import tpu as pltpu
from jax.sharding import PartitionSpec as P

MESH = pl.DeviceIdType.MESH

NDN = 8
KRYLOV = 3
EPS = 1e-06
SERIES_ORDER = 3
STEP_SIZE = 0.5
VMEM_LIMIT = 63 * 2**20
SHRINK = 2.0**-12
AHEAD = 20
AHEAD_PARTS = 4
PAIRS = ((0, 0), (0, 1), (0, 2), (0, 3), (1, 1), (1, 2), (1, 3), (2, 2), (2, 3))


def quadratic(gram, first, second):
    total = None
    for i, a in enumerate(first):
        if a is None:
            continue
        inner = None
        for j, b in enumerate(second):
            if b is None:
                continue
            piece = b * gram[(min(i, j), max(i, j))]
            inner = piece if inner is None else inner + piece
        total = a * inner if total is None else total + a * inner
    return total


def coefficients(sums, count):
    norm = sums[(0, 0)] * (1.0 / count) + EPS
    over = 1.0 / norm
    gram = {pair: value * (1.0 / count) * over for pair, value in sums.items()}
    eps = EPS * SHRINK * SHRINK
    a0 = gram[(0, 1)]
    rest = gram[(1, 1)] - 2.0 * a0 * gram[(0, 1)] + a0 * a0 * gram[(0, 0)]
    b1 = jnp.sqrt(jnp.maximum(rest, 0.0) + eps)
    i1 = 1.0 / b1
    v1 = (-a0 * i1, i1)
    w1 = (None, -a0 * i1, i1)
    a1 = quadratic(gram, v1, w1)
    r1 = (-a1 * v1[0] - b1, w1[1] - a1 * v1[1], w1[2])
    rest = quadratic(gram, r1, r1)
    b2 = jnp.sqrt(jnp.maximum(rest, 0.0) + eps)
    i2 = 1.0 / b2
    v2 = tuple(x * i2 for x in r1)
    a2 = quadratic(gram, v2, (None,) + v2)
    a0, a1, a2, b1, b2 = (x * (1.0 / SHRINK) for x in (a0, a1, a2, b1, b2))
    term = (jnp.ones_like(a0), jnp.zeros_like(a0), jnp.zeros_like(a0))
    c = term
    for order in range(1, SERIES_ORDER + 1):
        factor = -STEP_SIZE / order
        term = (
            (a0 * term[0] + b1 * term[1]) * factor,
            (b1 * term[0] + a1 * term[1] + b2 * term[2]) * factor,
            (b2 * term[1] + a2 * term[2]) * factor,
        )
        c = tuple(x + y for x, y in zip(c, term))
    size = jnp.sqrt(c[0] * c[0] + c[1] * c[1] + c[2] * c[2])
    scale = 1.0 / (size * jnp.sqrt(norm))
    return (
        (c[0] + c[1] * v1[0] + c[2] * v2[0]) * scale,
        (c[1] * v1[1] + c[2] * v2[1]) * scale,
        c[2] * v2[2] * scale,
    )


def kernel(
    segs, sectors, kinds_in, rows_in, psi, left, right, out,
    kinds, rows, start_v, r_v, l_v, z_v, src_0, src_1, src_2, src_3, src_4, src_5, u, r_prev, first_prev, env_out, env_in, table, red,
    load_sem, ex_send, ex_recv, red_send, red_recv, ahead_send, ahead_recv, env_send, env_recv, hello,
):
    src = (src_0, src_1, src_2, src_3, src_4, src_5)
    width, blk, cols = l_v.shape[0], l_v.shape[1], r_v.shape[2]
    grid_rows = sectors // NDN
    seg, sec = lax.axis_index("seg"), lax.axis_index("sec")
    row, col = sec // NDN, sec % NDN
    count = 1.0 * sectors * blk * cols

    def beside(rows_on):
        return (seg, lax.rem(row + rows_on + grid_rows, grid_rows) * NDN + col)

    def along(columns_on):
        return (seg, row * NDN + lax.rem(col + columns_on + NDN, NDN))

    loads = [
        pltpu.make_async_copy(psi, start_v, load_sem.at[0]),
        pltpu.make_async_copy(rows_in, rows, load_sem.at[1]),
        pltpu.make_async_copy(kinds_in, kinds, load_sem.at[2]),
        pltpu.make_async_copy(right, r_v, load_sem.at[3]),
        pltpu.make_async_copy(left, l_v, load_sem.at[4]),
    ]
    loads[0].start()
    loads[1].start()

    barrier = pltpu.get_barrier_semaphore()
    for on in (-1, 1):
        pl.semaphore_signal(barrier, inc=1, device_id=beside(on), device_id_type=MESH)
        pl.semaphore_signal(barrier, inc=1, device_id=along(on), device_id_type=MESH)
    before = lax.rem(seg + segs - 1, segs)
    pl.semaphore_signal(barrier, inc=1, device_id=(before, sec), device_id_type=MESH)

    for load in loads[2:]:
        load.start()
    loads[0].wait()
    loads[1].wait()
    live = lax.broadcasted_iota(jnp.int32, (blk, cols), 0) < rows[0, 0]
    start = jnp.where(live, start_v[...], 0.0)
    src[0][0] = start.astype(jnp.bfloat16)

    pl.semaphore_wait(barrier, 4 + 1)

    neighbours = (
        (1, 1, col < NDN - 1),
        (2, -1, col > 0),
        (3, NDN, row < grid_rows - 1),
        (4, -NDN, row > 0),
    )
    mirrored = {1: col > 0, 2: col < NDN - 1, 3: row > 0, 4: row < grid_rows - 1}

    def sending(step, kind, offset):
        return pltpu.make_async_remote_copy(
            src_ref=src[step].at[0],
            dst_ref=src[step].at[kind],
            send_sem=ex_send.at[step, kind],
            recv_sem=ex_recv.at[step, kind],
            device_id=(seg, sec - offset),
            device_id_type=MESH,
        )

    low, high = NDN // 2 - 1, NDN // 2
    inside = {1: jnp.logical_and(col > 0, col != high), 2: jnp.logical_and(col < NDN - 1, col != low)}

    def exchange_start(step):
        order = (
            (1, 1, col == high), (2, -1, col == low), (3, NDN, mirrored[3]), (4, -NDN, mirrored[4]),
            (1, 1, inside[1]), (2, -1, inside[2]),
        )
        for kind, offset, there in order:

            @pl.when(there)
            def _():
                sending(step, kind, offset).start()

    def exchange_wait(step):
        for kind, offset, there in neighbours:

            @pl.when(there)
            def _():
                sending(step, kind, offset).wait_recv()

    def exchange_drain(step):
        for kind, offset, _ in neighbours:

            @pl.when(mirrored[kind])
            def _():
                sending(step, kind, offset).wait_send()

    rounds = ((1, True), (2, True), (1, False), (2, False), (1, False))

    def hello_start(turn):
        stride, both = rounds[turn]
        for on in (-stride, stride):
            pl.semaphore_signal(hello.at[turn], inc=1, device_id=beside(on), device_id_type=MESH)
            if both:
                pl.semaphore_signal(hello.at[turn], inc=1, device_id=along(on), device_id_type=MESH)

    def hello_wait(turn):
        pl.semaphore_wait(hello.at[turn], 4 if rounds[turn][1] else 2)

    def hello_next(turn):
        hello_wait(turn)
        if turn + 1 < len(rounds):
            hello_start(turn + 1)

    def right_side(step):
        for w in range(width):
            source = src[step][kinds[w]]
            z_v[w * blk : (w + 1) * blk, :] = jnp.dot(
                source, r_v[w], preferred_element_type=jnp.float32
            ).astype(jnp.bfloat16)

    def left_side():
        total = jnp.zeros((blk, cols), jnp.float32)
        for w in range(0, width, 2):
            pair = jnp.concatenate([l_v[w], l_v[w + 1]], axis=1)
            total = total + jnp.dot(
                pair, z_v[w * blk : (w + 2) * blk, :], preferred_element_type=jnp.float32
            )
        keep = lax.broadcasted_iota(jnp.int32, (blk, cols), 0) < rows[0, 0]
        return total * jnp.where(keep, SHRINK, 0.0)

    def products(last):
        for k, (i, j) in enumerate(PAIRS):
            if j == last:
                product = u[i] * u[j]
                product = product[:, :128] + product[:, 128:]
                table[k : k + 1, :] = jnp.sum(product, axis=0, keepdims=True)

    lanes = lax.broadcasted_iota(jnp.int32, (16, 128), 1)
    sublanes = lax.broadcasted_iota(jnp.int32, (16, 128), 0)

    def reduce(update):
        buffer = red.at[update]
        totals = jnp.sum(table[...], axis=1, keepdims=True)
        mine = jnp.sum(jnp.where(lanes == sublanes, totals, 0.0), axis=0, keepdims=True)
        buffer[pl.ds(sec, 1), :] = mine

        def pass_on(turn, carry):
            far = (turn + 1) // 2
            offset = sectors // 2 + far - 2 * far * lax.rem(turn, 2)
            pltpu.make_async_remote_copy(
                src_ref=buffer.at[pl.ds(sec, 1), :],
                dst_ref=buffer.at[pl.ds(sec, 1), :],
                send_sem=red_send.at[update],
                recv_sem=red_recv.at[update],
                device_id=(seg, lax.rem(sec + offset, sectors)),
                device_id_type=MESH,
            ).start()
            return carry

        lax.fori_loop(0, sectors - 1, pass_on, 0)
        others = buffer.at[pl.ds(0, sectors - 1), :]
        every = pltpu.make_async_remote_copy(
            src_ref=others, dst_ref=others, send_sem=red_send.at[update], recv_sem=red_recv.at[update],
            device_id=(seg, lax.rem(sec + 1, sectors)), device_id_type=MESH,
        )
        every.wait_recv()
        every.wait_send()
        total = jnp.sum(buffer[...], axis=0, keepdims=True)
        spread = jnp.where(lanes == sublanes, jnp.broadcast_to(total, (16, 128)), 0.0)
        totals = jnp.broadcast_to(jnp.sum(spread, axis=1, keepdims=True), (16, 128))
        return {pair: totals[k : k + 1, :] for k, pair in enumerate(PAIRS)}

    def widen(coefficient):
        return jnp.concatenate([coefficient] * (cols // 128), axis=1)

    following = (lax.rem(seg + 1, segs), sec)
    ahead = min(AHEAD, width - 2)
    bounds = [ahead * part // AHEAD_PARTS for part in range(AHEAD_PARTS + 1)]

    def passing_right(part):
        piece = pl.ds(bounds[part], bounds[part + 1] - bounds[part])
        return pltpu.make_async_remote_copy(
            src_ref=right.at[piece], dst_ref=r_prev.at[piece],
            send_sem=ahead_send.at[part], recv_sem=ahead_recv.at[part],
            device_id=following, device_id_type=MESH,
        )

    def passing_first():
        return pltpu.make_async_remote_copy(
            src_ref=src[3].at[0], dst_ref=first_prev, send_sem=env_send.at[0], recv_sem=env_recv.at[0],
            device_id=following, device_id_type=MESH,
        )

    def passing_env():
        return pltpu.make_async_remote_copy(
            src_ref=env_out, dst_ref=env_in, send_sem=env_send.at[1], recv_sem=env_recv.at[1],
            device_id=following, device_id_type=MESH,
        )

    def boundary(vector, block):
        projected = jnp.dot(vector, block, preferred_element_type=jnp.float32).astype(jnp.bfloat16)
        env = lax.dot_general(projected, vector, (((1,), (1,)), ((), ())), preferred_element_type=jnp.float32)
        return (env * (cols * blk * width) ** (-0.5)).astype(jnp.bfloat16)

    exchange_start(0)

    @pl.when(seg < segs - 1)
    def _():
        for part in range(AHEAD_PARTS):
            passing_right(part).start()

    hello_start(0)
    u[0] = start
    table[...] = jnp.zeros(table.shape, table.dtype)
    products(0)
    for kind, _, there in neighbours:

        @pl.when(jnp.logical_not(there))
        def _():
            for step in (0, 1, 2, 4, 5):
                src[step][kind] = jnp.zeros((blk, cols), jnp.bfloat16)

    for load in loads[2:]:
        load.wait()

    for step in range(KRYLOV):
        hello_next(2 * step)
        exchange_wait(step)
        right_side(step)
        image = left_side()
        if step + 1 < KRYLOV:
            src[step + 1][0] = image.astype(jnp.bfloat16)
            exchange_start(step + 1)
            hello_next(2 * step + 1)
        u[step + 1] = image
        products(step + 1)

    mix = [widen(x) for x in coefficients(reduce(0), count)]
    first = mix[0] * u[0] + mix[1] * u[1] + mix[2] * u[2]
    first_bf = first.astype(jnp.bfloat16)

    src[3][0] = first_bf

    @pl.when(seg < segs - 1)
    def _():
        passing_first().start()
        for w in range(ahead, width):
            env_out[w - ahead] = boundary(first_bf, r_v[w])
        passing_env().start()

    for kind in range(1, 5):
        mixed = mix[0] * src[0][kind].astype(jnp.float32)
        mixed = mixed + mix[1] * src[1][kind].astype(jnp.float32)
        mixed = mixed + mix[2] * src[2][kind].astype(jnp.float32)
        src[3][kind] = mixed.astype(jnp.bfloat16)
    u[0] = first
    right_side(3)
    products(0)

    @pl.when(seg > 0)
    def _():
        for part in range(AHEAD_PARTS):
            passing_right(part).wait_recv()
        passing_first().wait_recv()
        vector = first_prev[...]
        for w in range(ahead):
            env = boundary(vector, r_prev[w])
            l_v[w] = (l_v[w].astype(jnp.float32) + env.astype(jnp.float32)).astype(jnp.bfloat16)
        passing_env().wait_recv()
        for w in range(ahead, width):
            env = env_in[w - ahead]
            l_v[w] = (l_v[w].astype(jnp.float32) + env.astype(jnp.float32)).astype(jnp.bfloat16)

    for step in range(KRYLOV):
        if step > 0:
            exchange_wait(step + 3)
            right_side(step + 3)
        image = left_side()
        if step + 1 < KRYLOV:
            src[step + 4][0] = image.astype(jnp.bfloat16)
            exchange_start(step + 4)
        u[step + 1] = image
        products(step + 1)

    mix = [widen(x) for x in coefficients(reduce(1), count)]
    out[...] = mix[0] * u[0] + mix[1] * u[1] + mix[2] * u[2]

    for step in (0, 1, 2, 4, 5):
        exchange_drain(step)

    @pl.when(seg < segs - 1)
    def _():
        for part in range(AHEAD_PARTS):
            passing_right(part).wait_send()
        passing_first().wait_send()
        passing_env().wait_send()


def per_device(segs, sectors, psi, left_env, right_env, term_kind, block_rows):
    _, blk, cols = psi.shape
    width = left_env.shape[1]
    ahead = min(AHEAD, width - 2)
    anywhere = pl.BlockSpec(memory_space=pltpu.HBM)
    result = pl.pallas_call(
        functools.partial(kernel, segs, sectors),
        out_shape=pltpu.VMEM((blk, cols), jnp.float32),
        in_specs=[anywhere] * 5,
        out_specs=pl.BlockSpec(memory_space=pltpu.VMEM),
        scratch_shapes=[
            pltpu.SMEM((width,), jnp.int32),
            pltpu.SMEM((1, 1), jnp.int32),
            pltpu.VMEM((blk, cols), jnp.float32),
            pltpu.VMEM((width, cols, cols), jnp.bfloat16),
            pltpu.VMEM((width, blk, blk), jnp.bfloat16),
            pltpu.VMEM((width * blk, cols), jnp.bfloat16),
            *[pltpu.VMEM((5, blk, cols), jnp.bfloat16) for _ in range(6)],
            pltpu.VMEM((KRYLOV + 1, blk, cols), jnp.float32),
            pltpu.VMEM((ahead, cols, cols), jnp.bfloat16),
            pltpu.VMEM((blk, cols), jnp.bfloat16),
            pltpu.VMEM((width - ahead, blk, blk), jnp.bfloat16),
            pltpu.VMEM((width - ahead, blk, blk), jnp.bfloat16),
            pltpu.VMEM((16, 128), jnp.float32),
            pltpu.VMEM((2, sectors, 128), jnp.float32),
            pltpu.SemaphoreType.DMA((5,)),
            pltpu.SemaphoreType.DMA((6, 5)),
            pltpu.SemaphoreType.DMA((6, 5)),
            pltpu.SemaphoreType.DMA((2,)),
            pltpu.SemaphoreType.DMA((2,)),
            pltpu.SemaphoreType.DMA((AHEAD_PARTS,)),
            pltpu.SemaphoreType.DMA((AHEAD_PARTS,)),
            pltpu.SemaphoreType.DMA((2,)),
            pltpu.SemaphoreType.DMA((2,)),
            pltpu.SemaphoreType.REGULAR((5,)),
        ],
        compiler_params=pltpu.CompilerParams(
            collective_id=0, has_side_effects=True, vmem_limit_bytes=VMEM_LIMIT
        ),
    )(term_kind, block_rows, psi[0], left_env[0], right_env[0])
    return result[None]


def solution(mesh):
    in_specs = (
        P("seg", "sec", None),
        P("seg", None, "sec", None),
        P("seg", None, None, None),
        P(),
        P("seg", "sec"),
    )
    out_specs = P("seg", "sec", None)
    return jax.shard_map(
        functools.partial(per_device, mesh.shape["seg"], mesh.shape["sec"]),
        mesh=mesh, in_specs=in_specs, out_specs=out_specs, check_vma=False,
    )
```
